32 devices in a mesh: replica: 8 (over y, x, core), fsdp: 4 (over z).
Axes of the slice: x: 2, y: 2, z: 4, core: 2. Of those that a mesh axis runs over, the one named last changes fastest.
Arguments:
- tokens: bfloat16 [16384, 4096], P(('replica', 'fsdp')), may hold values from -6 to 6
- key_cotangent: bfloat16 [16384, 512], P(('replica', 'fsdp')), may hold values from -0.25 to 0.25
- key_weight: bfloat16 [32768, 512], P(('replica', 'fsdp')), may hold values from -0.09375 to 0.09375
- first_moment: float32 [32768, 512], P(('replica', 'fsdp')), may hold values from -6 to 6
- second_moment: float32 [32768, 512], P(('replica', 'fsdp')), may hold values from 0.1 to 3
- local_slab: bfloat16 [6144, 4096], P(('replica', 'fsdp')), as said below
- outer_params: float32 [768, 4096], P('fsdp', 'replica')
- outer_momentum: float32 [768, 4096], P('fsdp', 'replica'), may hold values from -3 to 3
Outputs:
- projected: bfloat16 [16384, 512], P(('replica', 'fsdp'))
- new_weight: bfloat16 [32768, 512], P(('replica', 'fsdp'))
- new_first: float32 [32768, 512], P(('replica', 'fsdp'))
- new_second: float32 [32768, 512], P(('replica', 'fsdp'))
- new_outer: float32 [768, 4096], P('fsdp', 'replica')
- new_momentum: float32 [768, 4096], P('fsdp', 'replica')
- new_local: bfloat16 [6144, 4096], P(('replica', 'fsdp'))
The draws below stay inside these ranges and needn't reach their ends.
Inputs may be any that keep to these rules, and one draw needn't show every extreme that they name: `local_slab`: each replica's fragment equals outer_params plus a drift that the replicas partly share.
All inputs are finite; a program needn't handle non-finite values.
Results may differ from the reference program's by a relative error of at most 0.00045.
Values may be sent and summed in bfloat16 or wider, within the bound.
No kernel may reach another device: no remote copies, remote signals or barrier semaphores. Data moves between devices by JAX's collectives and lax.ppermute only.
A program may use at most 128 MiB of HBM per device.

```python
import math
import jax
import jax.numpy as jnp
from jax import lax

D = 4096
KEY_WIDTH = 512
REPLICAS = 8
REP_TOKENS = 2048
TOKENS = 16384
FRAG = 768


def shared_base(key):
    return jax.random.normal(jax.random.fold_in(key, 11), (FRAG, D), jnp.float32)


def draw_outer_params(key, part):
    return shared_base(key)


def draw_local_slab(key, part):
    base = shared_base(key)
    common = 0.5 * jax.random.normal(jax.random.fold_in(key, 12), (FRAG, D), jnp.float32)
    spread = 0.3 * jax.random.normal(jax.random.fold_in(key, 13), (REPLICAS, FRAG, D), jnp.float32)
    slabs = base[None] + common[None] + spread
    return slabs.reshape(REPLICAS * FRAG, D).astype(jnp.bfloat16)


def block_scale(own_key, dims, split, smallest, largest):
    level, own = 1.0, jax.random.fold_in(own_key, 6)
    for dim, shards_of in split:
        steps = jnp.exp(jax.random.uniform(jax.random.fold_in(own, dim), (shards_of,), jnp.float32, smallest / len(split), largest / len(split)))
        level = level * jnp.repeat(steps, dims[dim] // shards_of).reshape([-1 if axis == dim else 1 for axis in range(len(dims))])
    return level


def normal_values(stream_key, dims, deviation, bound, split=(), kind=jnp.bfloat16):
    entries = jax.random.normal(stream_key, dims, jnp.float32) * deviation
    if len(split) > 0:
        entries = block_scale(stream_key, dims, split, -0.22, 0.18) * entries
    return jnp.clip(entries, min=-bound, max=bound).astype(kind)


def setup_inputs(seed: int = 0) -> dict:
    splits = jax.random.split(jax.random.key(seed), 9)
    tokens = normal_values(splits[0], (TOKENS, D), 1.0, 6.0, ((0, 32),))
    key_cotangent = normal_values(splits[1], (TOKENS, KEY_WIDTH), (REP_TOKENS // 4) ** -0.5, 0.25, ((0, 32),))
    key_weight = normal_values(splits[2], (REPLICAS * D, KEY_WIDTH), D ** -0.5, 0.09375, ((0, 32),))
    first_moment = normal_values(splits[3], (REPLICAS * D, KEY_WIDTH), 1.0, 6.0, ((0, 32),), jnp.float32)
    second_moment = jnp.clip(jnp.exp(math.log(3.0) - 3.4011974 * jax.random.uniform(splits[4], (REPLICAS * D, KEY_WIDTH), jnp.float32) ** block_scale(splits[4], (REPLICAS * D, KEY_WIDTH), ((0, 32),), -0.2, 0.2)), 0.1, 3.0)
    local_slab = draw_local_slab(jax.random.fold_in(splits[8], 71), 0)
    outer_params = draw_outer_params(jax.random.fold_in(splits[8], 71), 0)
    outer_momentum = normal_values(splits[7], (FRAG, D), 0.5, 3.0, ((0, 4), (1, 8)), jnp.float32)
    return dict(tokens=tokens, key_cotangent=key_cotangent, key_weight=key_weight, first_moment=first_moment, second_moment=second_moment, local_slab=local_slab, outer_params=outer_params, outer_momentum=outer_momentum)


BETA_ONE = 0.9
BETA_TWO = 0.95
INNER_RATE = 0.001
DECAY_RATE = 0.1
EPSILON = 1e-08
FIRST_FIX = 1.0 - (0.9 ** 50) ** 2
SECOND_FIX = 1.0 - (0.95 ** 50) ** 2
OUTER_RATE = 0.7
OUTER_MOMENTUM = 0.9
MERGE_WEIGHT = 0.5

def reference(tokens, key_cotangent, key_weight, first_moment, second_moment, local_slab, outer_params, outer_momentum):
    rep_tokens = tokens.reshape(REPLICAS, REP_TOKENS, D)
    rep_cot = key_cotangent.reshape(REPLICAS, REP_TOKENS, KEY_WIDTH)
    rep_weight = key_weight.reshape(REPLICAS, D, KEY_WIDTH)

    def one_replica(index):
        inputs = rep_tokens[index]
        keyed = jnp.dot(inputs, rep_weight[index], preferred_element_type=jnp.float32).astype(jnp.bfloat16)
        gradient = lax.dot_general(inputs, rep_cot[index], (((0,), (0,)), ((), ())), preferred_element_type=jnp.float32)
        return (keyed, gradient)
    projected, gradient = lax.map(one_replica, jnp.arange(REPLICAS, dtype=jnp.int32))
    projected = projected.reshape(TOKENS, KEY_WIDTH)
    gradient = gradient.reshape(REPLICAS * D, KEY_WIDTH)
    new_first = BETA_ONE * first_moment + (1.0 - BETA_ONE) * gradient
    new_second = BETA_TWO * second_moment + (1.0 - BETA_TWO) * gradient * gradient
    weight_f = key_weight.astype(jnp.float32)
    update = new_first / FIRST_FIX / (jnp.sqrt(new_second / SECOND_FIX) + EPSILON) + DECAY_RATE * weight_f
    new_weight = (weight_f - INNER_RATE * update).astype(jnp.bfloat16)
    slabs = local_slab.reshape(REPLICAS, FRAG, D).astype(jnp.float32)
    average = lax.optimization_barrier(jnp.sum(slabs, axis=0)) / REPLICAS
    pseudo_grad = outer_params - average
    new_momentum = OUTER_MOMENTUM * outer_momentum + pseudo_grad
    new_outer = outer_params - OUTER_RATE * (pseudo_grad + OUTER_MOMENTUM * new_momentum)
    merged = MERGE_WEIGHT * slabs + (1.0 - MERGE_WEIGHT) * new_outer[None]
    new_local = merged.astype(jnp.bfloat16).reshape(REPLICAS * FRAG, D)
    return (projected, new_weight, new_first, new_second, new_outer, new_momentum, new_local)
```

```python
import jax
import jax.numpy as jnp
from jax import lax
from jax.sharding import PartitionSpec as P

BETA_ONE = 0.9
BETA_TWO = 0.95
INNER_RATE = 0.001
DECAY_RATE = 0.1
EPSILON = 1e-08
FIRST_FIX = 1.0 - (0.9**50) ** 2
SECOND_FIX = 1.0 - (0.95**50) ** 2
OUTER_RATE = 0.7
OUTER_MOMENTUM = 0.9
MERGE_WEIGHT = 0.5


def term_scale(replica_tokens):
    scale = 1.0
    while replica_tokens * 6 * 0.25 * scale * 2 < 60000:
        scale *= 2
    return scale


def outer_update(outer_params, outer_momentum, summed, replicas):
    average = summed / replicas
    pseudo_grad = outer_params - average
    new_momentum = OUTER_MOMENTUM * outer_momentum + pseudo_grad
    new_outer = outer_params - OUTER_RATE * (pseudo_grad + OUTER_MOMENTUM * new_momentum)
    return (new_outer, new_momentum)


def shards(
    tokens,
    key_cotangent,
    key_weight,
    first_moment,
    second_moment,
    local_slab,
    outer_params,
    outer_momentum,
):
    n = lax.axis_size("fsdp")
    me = lax.axis_index("fsdp")
    rows = key_weight.shape[0]
    scale = term_scale(n * tokens.shape[0])

    def columns_of(owner):
        return lax.dynamic_slice_in_dim(tokens, jnp.clip(owner, 0, n - 1) * rows, rows, 1)

    def term(owner):
        return lax.dot_general(
            columns_of(owner),
            key_cotangent,
            (((0,), (0,)), ((), ())),
            preferred_element_type=jnp.float32,
        )

    def keyed(owner, weight):
        return jnp.dot(columns_of(owner), weight, preferred_element_type=jnp.float32)

    held_up, held_down = key_weight, key_weight
    total = keyed(me, key_weight)
    come_up, come_down = None, None
    for t in range(n - 1):
        up = [(i, i + 1) for i in range(t, n - 1)]
        down = [(n - 1 - a, n - 1 - b) for a, b in up]
        held_up = lax.ppermute(held_up, "fsdp", up)
        held_down = lax.ppermute(held_down, "fsdp", down)
        total = total + keyed(me - t - 1, held_up) + keyed(me + t + 1, held_down)
        send_up = term(n - 1 - t + me) * scale
        send_down = term(t - (n - 1 - me)) * scale
        if come_up is not None:
            send_up = send_up + come_up.astype(jnp.float32)
            send_down = send_down + come_down.astype(jnp.float32)
        up = [(i, i + 1) for i in range(t + 1)]
        down = [(n - 1 - a, n - 1 - b) for a, b in up]
        come_up = lax.ppermute(send_up.astype(jnp.float16), "fsdp", up)
        come_down = lax.ppermute(send_down.astype(jnp.float16), "fsdp", down)
    projected = total.astype(jnp.bfloat16)
    gradient = term(me)
    if come_up is not None:
        gradient = gradient + (come_up.astype(jnp.float32) + come_down.astype(jnp.float32)) / scale

    new_first = BETA_ONE * first_moment + (1.0 - BETA_ONE) * gradient
    new_second = BETA_TWO * second_moment + (1.0 - BETA_TWO) * gradient * gradient
    weight_f = key_weight.astype(jnp.float32)
    update = (
        new_first / FIRST_FIX / (jnp.sqrt(new_second / SECOND_FIX) + EPSILON)
        + DECAY_RATE * weight_f
    )
    new_weight = (weight_f - INNER_RATE * update).astype(jnp.bfloat16)

    replicas = lax.axis_size("replica")
    slab_rows, column_count = outer_params.shape
    parts = lax.all_to_all(
        local_slab.reshape(slab_rows, replicas, column_count), "replica", 1, 0, tiled=False
    )
    summed = jnp.sum(parts.astype(jnp.float32), axis=0)
    new_outer, new_momentum = outer_update(outer_params, outer_momentum, summed, replicas)
    whole_outer = lax.all_gather(new_outer, "replica", axis=1, tiled=True)
    slab_f = local_slab.astype(jnp.float32)
    new_local = (MERGE_WEIGHT * slab_f + (1.0 - MERGE_WEIGHT) * whole_outer).astype(jnp.bfloat16)
    return (projected, new_weight, new_first, new_second, new_outer, new_momentum, new_local)


def solution(mesh):
    split = P(("replica", "fsdp"), None)
    outer = P("fsdp", "replica")
    return jax.shard_map(
        shards,
        mesh=mesh,
        in_specs=(split, split, split, split, split, split, outer, outer),
        out_specs=(split, split, split, split, outer, outer, split),
        check_vma=False,
    )
```

```python
import functools

import jax
import jax.numpy as jnp
from jax import lax
from jax.experimental import pallas as pl
from jax.experimental.pallas import tpu as pltpu
from jax.sharding import PartitionSpec as P

BETA_ONE = 0.9
BETA_TWO = 0.95
INNER_RATE = 0.001
DECAY_RATE = 0.1
EPSILON = 1e-08
FIRST_FIX = 1.0 - (0.9**50) ** 2
SECOND_FIX = 1.0 - (0.95**50) ** 2
OUTER_RATE = 0.7
OUTER_MOMENTUM = 0.9
MERGE_WEIGHT = 0.5
PIECES = 2
WEIGHT_PIECES = 1
TUNE = {'vmem': 60, 'columns': 40000000000, 'outer_after': (3, 0), ('x', 2, 0): 10, ('x', 2, 1): 10, ('x', 3, 0): 10, ('x', 3, 1): 10}
VM = TUNE.get('vmem', 60)
ANY = pl.BlockSpec(memory_space=pl.ANY)
MIB = 1 << 20


def term_scale(replica_tokens):
    scale = 1.0
    while replica_tokens * 6 * 0.25 * scale * 2 < 60000:
        scale *= 2
    return scale


def shape_of(array, dtype=None):
    return jax.ShapeDtypeStruct(array.shape, dtype or array.dtype)


def call(kernel, vmem=VM, flops=0, moved=0, **settings):
    return pl.pallas_call(
        kernel,
        compiler_params=pltpu.CompilerParams(vmem_limit_bytes=vmem * MIB),
        cost_estimate=pl.CostEstimate(flops=flops, bytes_accessed=moved, transcendentals=0),
        **settings,
    )


def after(value, *others, flops=0):
    def kernel(*refs):
        pass

    return call(
        kernel,
        vmem=1,
        flops=flops,
        out_shape=shape_of(value),
        in_specs=[ANY] * (1 + len(others)),
        out_specs=ANY,
        input_output_aliases={0: 0},
    )(value, *others)


def gradient_terms(owners, tokens, key_cotangent, scale, rows, strips, *others):
    units = owners.shape[0]
    strip, width = rows // strips, key_cotangent.shape[1]

    def kernel(owners_ref, tokens_ref, cotangent_ref, *refs):
        outs = refs[len(others) : len(others) + units * strips]
        made, sems = refs[-2:]
        unit = pl.program_id(0)
        slot = lax.rem(unit, 2)

        def copy(slot, s, k):
            return pltpu.make_async_copy(made.at[slot, s], outs[k * strips + s], sems.at[slot, s])

        @pl.when(unit >= 2)
        def _():
            for s in range(strips):
                copy(slot, s, 0).wait()

        for s in range(strips):
            made[slot, s] = scale * lax.dot_general(
                tokens_ref[:, s * strip : (s + 1) * strip],
                cotangent_ref[...],
                (((0,), (0,)), ((), ())),
                preferred_element_type=jnp.float32,
            )
        for k in range(units):

            @pl.when(unit == k)
            def _(k=k):
                for s in range(strips):
                    copy(slot, s, k).start()

        @pl.when(unit == units - 1)
        def _():
            for s in range(strips):
                if units > 1:
                    copy(1 - slot, s, 0).wait()
                copy(slot, s, 0).wait()

    outs = call(
        kernel,
        flops=TUNE.get("terms", 5) * 10**9,
        out_shape=[jax.ShapeDtypeStruct((strip, width), jnp.float32)] * (units * strips),
        grid_spec=pltpu.PrefetchScalarGridSpec(
            num_scalar_prefetch=1,
            grid=(units,),
            in_specs=[
                pl.BlockSpec((tokens.shape[0], rows), lambda i, owners: (0, owners[i])),
                pl.BlockSpec(key_cotangent.shape, lambda i, owners: (0, 0)),
            ]
            + [ANY] * len(others),
            out_specs=[ANY] * (units * strips),
            scratch_shapes=[
                pltpu.VMEM((2, strips, strip, width), jnp.float32),
                pltpu.SemaphoreType.DMA((2, strips)),
            ],
        ),
    )(owners, tokens, key_cotangent, *others)
    return [outs[k * strips : (k + 1) * strips] for k in range(units)]


def project(owners, valid, tokens, weights, rows, *others):
    strip, width = weights[0][0].shape
    strips = rows // strip
    steps = len(weights)
    flat = [piece for step in weights for piece in step]
    count = len(flat)

    def kernel(owners_ref, valid_ref, tokens_ref, *refs):
        out, total, held, sems = refs[-4:]
        step = pl.program_id(0)

        def copy(k, s):
            return pltpu.make_async_copy(refs[k * strips + s], held.at[k, s], sems.at[k, s])

        @pl.when(step == 0)
        def _():
            for k in range(steps):

                @pl.when(valid_ref[k] == 1)
                def _(k=k):
                    for s in range(strips):
                        copy(k, s).start()

            total[...] = jnp.zeros_like(total)

        @pl.when(valid_ref[step] == 1)
        def _():
            for s in range(strips):
                pltpu.make_async_copy(refs[s], held.at[step, s], sems.at[step, s]).wait()
                total[...] += jnp.dot(
                    tokens_ref[:, s * strip : (s + 1) * strip],
                    held[step, s],
                    preferred_element_type=jnp.float32,
                )

        @pl.when(step == steps - 1)
        def _():
            out[...] = total[...].astype(out.dtype)

    return call(
        kernel,
        flops=TUNE.get("project", 6) * 10**9,
        out_shape=jax.ShapeDtypeStruct((tokens.shape[0], width), jnp.bfloat16),
        grid_spec=pltpu.PrefetchScalarGridSpec(
            num_scalar_prefetch=2,
            grid=(steps,),
            in_specs=[pl.BlockSpec((tokens.shape[0], rows), lambda i, o, v: (0, o[i]))]
            + [ANY] * (count + len(others)),
            out_specs=pl.BlockSpec((tokens.shape[0], width), lambda i, o, v: (0, 0)),
            scratch_shapes=[
                pltpu.VMEM((tokens.shape[0], width), jnp.float32),
                pltpu.VMEM((steps, strips, strip, width), jnp.bfloat16),
                pltpu.SemaphoreType.DMA((steps, strips)),
            ],
        ),
    )(owners, valid, tokens, *flat, *others)


def row_blocks(slab_rows):
    return next(k for k in (4, 3, 2, 1) if slab_rows % (16 * k) == 0 or k == 1)


def outer_terms(slab, outer_params, outer_momentum, place, replicas, *others):
    slab_rows, column_count = outer_params.shape
    blocks = row_blocks(slab_rows)
    step = slab_rows // blocks
    both_ways = OUTER_RATE * (1.0 + OUTER_MOMENTUM)

    def kernel(place_ref, slab_ref, params_ref, momentum_ref, *refs):
        out_ref = refs[-1]
        for r in range(replicas):
            part = slab_ref[:, r * column_count : (r + 1) * column_count]
            out_ref[r] = (both_ways / replicas) * part.astype(jnp.float32)
        own = (1.0 - both_ways) * params_ref[...]
        own = own - (OUTER_RATE * OUTER_MOMENTUM * OUTER_MOMENTUM) * momentum_ref[...]
        out_ref[place_ref[0]] += own

    rows_of = pl.BlockSpec((step, column_count), lambda i, place: (i, 0))
    return call(
        kernel,
        flops=TUNE.get("columns", 0),
        out_shape=jax.ShapeDtypeStruct((replicas, slab_rows, column_count), jnp.float32),
        grid_spec=pltpu.PrefetchScalarGridSpec(
            num_scalar_prefetch=1,
            grid=(blocks,),
            in_specs=[pl.BlockSpec((step, slab.shape[1]), lambda i, place: (i, 0)), rows_of, rows_of]
            + [ANY] * len(others),
            out_specs=pl.BlockSpec((replicas, step, column_count), lambda i, place: (0, i, 0)),
        ),
    )(jnp.reshape(place, (1,)).astype(jnp.int32), slab, outer_params, outer_momentum, *others)


def merge(slab, whole_outer, *others):
    replicas, slab_rows, column_count = whole_outer.shape
    blocks = row_blocks(slab_rows)
    step = slab_rows // blocks

    def kernel(slab_ref, outer_ref, *refs):
        out_ref = refs[-1]
        for r in range(replicas):
            part = slice(r * column_count, (r + 1) * column_count)
            slab_f = slab_ref[:, part].astype(jnp.float32)
            merged = MERGE_WEIGHT * slab_f + (1.0 - MERGE_WEIGHT) * outer_ref[r]
            out_ref[:, part] = merged.astype(out_ref.dtype)

    block = pl.BlockSpec((step, slab.shape[1]), lambda i: (i, 0))
    return call(
        kernel,
        flops=TUNE.get("merge", 3) * 10**9,
        out_shape=shape_of(slab),
        grid=(blocks,),
        in_specs=[block, pl.BlockSpec((replicas, step, column_count), lambda i: (0, i, 0))]
        + [ANY] * len(others),
        out_specs=block,
    )(slab, whole_outer, *others)


def shards(
    tokens,
    key_cotangent,
    key_weight,
    first_moment,
    second_moment,
    local_slab,
    outer_params,
    outer_momentum,
):
    n = lax.axis_size("fsdp")
    me = lax.axis_index("fsdp")
    replicas = lax.axis_size("replica")
    rows = key_weight.shape[0]
    strip = rows // PIECES
    scale = term_scale(n * tokens.shape[0])
    every = range(PIECES)

    def mirrored(links):
        return [(n - 1 - a, n - 1 - b) for a, b in links]

    def among(devices):
        return functools.reduce(jnp.logical_or, [me == d for d in devices], jnp.bool_(False))

    def distinct(devices):
        return len(set(devices)) == len(devices)

    def exchange(up_load, down_load, up):
        down = mirrored(up)
        if distinct([a for a, _ in up + down]) and distinct([b for _, b in up + down]):
            load = up_load
            if up_load is not down_load:
                load = jnp.where(among([a for a, _ in up]), up_load, down_load)
            come = lax.ppermute(load, "fsdp", up + down)
            return come, come
        return lax.ppermute(up_load, "fsdp", up), lax.ppermute(down_load, "fsdp", down)

    def one_of(come):
        return come[0].astype(jnp.float32) if come[0] is come[1] else both(come)

    def both(come):
        return come[0].astype(jnp.float32) + come[1].astype(jnp.float32)

    weight_strip = rows // WEIGHT_PIECES
    each = range(WEIGHT_PIECES)
    weights = [key_weight[p * weight_strip : (p + 1) * weight_strip] for p in each]
    held = [[None] * WEIGHT_PIECES for _ in range(n)]
    sums = [None] * PIECES

    for p in each:
        held[0][p] = exchange(weights[p], weights[p], [(i, i + 1) for i in range(n - 1)])
    place = lax.axis_index("replica")

    owners, loads_of = [], [None]
    for t in range(1, n):
        up, down = n + me - t, t - 1 - (n - 1 - me)
        if 2 * t <= n:
            loads_of.append([len(owners)])
            owners.append(jnp.where(me < t, up, down))
        else:
            loads_of.append([len(owners), len(owners) + 1])
            owners += [up, down]
    owners = jnp.clip(jnp.stack(owners), 0, n - 1).astype(jnp.int32)
    terms = gradient_terms(owners, tokens, key_cotangent, scale, rows, PIECES)
    others = (terms[0][0],) if TUNE.get("terms_first", 1) else ()
    columns = outer_terms(local_slab, outer_params, outer_momentum, place, replicas, *others)
    new_outer = lax.psum_scatter(columns, "replica", scatter_dimension=0, tiled=False)


    for t in range(1, n):
        links = [(i, i + 1) for i in range(t)]
        for p in every:
            w = p * WEIGHT_PIECES // PIECES
            came = held[t - 1][w]
            if t < n - 1 and held[t][w] is None:
                held[t][w] = exchange(*came, [(i, i + 1) for i in range(t, n - 1)])
            if (t, p) == TUNE.get("outer_after"):
                new_outer = after(new_outer, *came)
            lag = TUNE.get("lag", 2)
            others = tuple(held[t - lag][w]) if t >= TUNE.get("tied_from", 3) and t >= lag else ()
            if (t, p) == TUNE.get("outer_before"):
                others = (*others, new_outer)
            loads = [terms[k][p] if t == 1 else after(terms[k][p], *others, flops=TUNE.get(("x", t, p), 0) * 10**9) for k in loads_of[t]]
            if len(loads) == 1:
                load = loads[0] if t == 1 else loads[0] + one_of(sums[p])
                up_load = down_load = load.astype(jnp.float16)
            else:
                up_load = (loads[0] + sums[p][0].astype(jnp.float32)).astype(jnp.float16)
                down_load = (loads[1] + sums[p][1].astype(jnp.float32)).astype(jnp.float16)
            sums[p] = exchange(up_load, down_load, links)
    whole_outer = lax.all_gather(new_outer, "replica", axis=0)
    new_momentum = (outer_params - new_outer) / OUTER_RATE + OUTER_MOMENTUM * outer_momentum
    new_momentum = new_momentum / (1.0 + OUTER_MOMENTUM)
    new_local = merge(local_slab, whole_outer, *((held[n - 2][WEIGHT_PIECES - 1][0],) if TUNE.get("merge_late", 0) else ()))

    owners, valid, steps = [me], [me >= 0], [weights]
    for t in range(n - 1):
        if held[t][0][0] is held[t][0][1]:
            owners.append(jnp.where(me - t - 1 >= 0, me - t - 1, me + t + 1))
            valid.append((me - t - 1 >= 0) | (me + t + 1 <= n - 1))
            steps.append([held[t][p][0] for p in each])
        else:
            owners += [me - t - 1, me + t + 1]
            valid += [me - t - 1 >= 0, me + t + 1 <= n - 1]
            steps += [[held[t][p][0] for p in each], [held[t][p][1] for p in each]]
    owners = jnp.clip(jnp.stack(owners), 0, n - 1).astype(jnp.int32)
    others = (new_local,) if TUNE.get("merge_first", 1) else ()
    projected = project(owners, jnp.stack(valid).astype(jnp.int32), tokens, steps, rows, *others)

    [own] = gradient_terms(jnp.reshape(me, (1,)), tokens, key_cotangent, scale, rows, PIECES, *others)
    own = [after(o, projected) for o in own]
    gradient = jnp.concatenate([own[p] + one_of(sums[p]) for p in every], 0) / scale
    new_first = BETA_ONE * first_moment + (1.0 - BETA_ONE) * gradient
    new_second = BETA_TWO * second_moment + (1.0 - BETA_TWO) * gradient * gradient
    weight_f = key_weight.astype(jnp.float32)
    update = (
        new_first / FIRST_FIX / (jnp.sqrt(new_second / SECOND_FIX) + EPSILON)
        + DECAY_RATE * weight_f
    )
    new_weight = (weight_f - INNER_RATE * update).astype(jnp.bfloat16)
    return (projected, new_weight, new_first, new_second, new_outer, new_momentum, new_local)


def solution(mesh):
    split = P(("replica", "fsdp"), None)
    outer = P("fsdp", "replica")
    return jax.shard_map(
        shards,
        mesh=mesh,
        in_specs=(split, split, split, split, split, split, outer, outer),
        out_specs=(split, split, split, split, outer, outer, split),
        check_vma=False,
    )
```

```python
import functools

import jax
import jax.numpy as jnp
from jax import lax
from jax.experimental import pallas as pl
from jax.experimental.pallas import tpu as pltpu
from jax.sharding import PartitionSpec as P

BETA_ONE = 0.9
BETA_TWO = 0.95
INNER_RATE = 0.001
DECAY_RATE = 0.1
EPSILON = 1e-08
FIRST_FIX = 1.0 - (0.9**50) ** 2
SECOND_FIX = 1.0 - (0.95**50) ** 2
OUTER_RATE = 0.7
OUTER_MOMENTUM = 0.9
MERGE_WEIGHT = 0.5
TUNE = {'rp': 2, 'gp': 2, 'vk': 16, 'vm': 12, 'vo': 12, 'columns': 0, 'chain': 1, 'gate': None, ('tie', 1, 0): None, ('tie', 1, 1): None, ('tie', 3, 0): 2, ('tie', 3, 1): 2, ('x', 2, 0): 14, ('x', 2, 1): 14, ('x', 3, 0): 14, ('x', 3, 1): 14}
PIECES = TUNE.get("rp", 2)
WEIGHT_PIECES = TUNE.get('gp', 2)
VM = TUNE.get('vmem', 60)
ANY = pl.BlockSpec(memory_space=pl.ANY)
MIB = 1 << 20


def term_scale(replica_tokens):
    scale = 1.0
    while replica_tokens * 6 * 0.25 * scale * 2 < 60000:
        scale *= 2
    return scale


def shape_of(array, dtype=None):
    return jax.ShapeDtypeStruct(array.shape, dtype or array.dtype)


def call(kernel, vmem=VM, flops=0, moved=0, **settings):
    return pl.pallas_call(
        kernel,
        compiler_params=pltpu.CompilerParams(vmem_limit_bytes=vmem * MIB),
        cost_estimate=pl.CostEstimate(flops=flops, bytes_accessed=moved, transcendentals=0),
        **settings,
    )


def after(value, *others, flops=0):
    def kernel(*refs):
        pass

    return call(
        kernel,
        vmem=1,
        flops=flops,
        out_shape=shape_of(value),
        in_specs=[ANY] * (1 + len(others)),
        out_specs=ANY,
        input_output_aliases={0: 0},
    )(value, *others)


def project(owners, valid, tokens, weights, rows, *others):
    strip, width = weights[0][0].shape
    strips = rows // strip
    steps = len(weights)
    flat = [piece for step in weights for piece in step]
    count = len(flat)

    def kernel(owners_ref, valid_ref, tokens_ref, *refs):
        out, total, held, sems = refs[-4:]
        step = pl.program_id(0)

        def copy(k, s):
            return pltpu.make_async_copy(refs[k * strips + s], held.at[k, s], sems.at[k, s])

        @pl.when(step == 0)
        def _():
            for k in range(steps):

                @pl.when(valid_ref[k] == 1)
                def _(k=k):
                    for s in range(strips):
                        copy(k, s).start()

            total[...] = jnp.zeros_like(total)

        @pl.when(valid_ref[step] == 1)
        def _():
            for s in range(strips):
                pltpu.make_async_copy(refs[s], held.at[step, s], sems.at[step, s]).wait()
                total[...] += jnp.dot(
                    tokens_ref[:, s * strip : (s + 1) * strip],
                    held[step, s],
                    preferred_element_type=jnp.float32,
                )

        @pl.when(step == steps - 1)
        def _():
            out[...] = total[...].astype(out.dtype)

    return call(
        kernel,
        vmem=TUNE.get('vk', 60),
        flops=TUNE.get("project", 6) * 10**9,
        out_shape=jax.ShapeDtypeStruct((tokens.shape[0], width), jnp.bfloat16),
        grid_spec=pltpu.PrefetchScalarGridSpec(
            num_scalar_prefetch=2,
            grid=(steps,),
            in_specs=[pl.BlockSpec((tokens.shape[0], rows), lambda i, o, v: (0, o[i]))]
            + [ANY] * (count + len(others)),
            out_specs=pl.BlockSpec((tokens.shape[0], width), lambda i, o, v: (0, 0)),
            scratch_shapes=[
                pltpu.VMEM((tokens.shape[0], width), jnp.float32),
                pltpu.VMEM((steps, strips, strip, width), jnp.bfloat16),
                pltpu.SemaphoreType.DMA((steps, strips)),
            ],
        ),
    )(owners, valid, tokens, *flat, *others)


def row_blocks(slab_rows):
    return next(k for k in (4, 3, 2, 1) if slab_rows % (16 * k) == 0 or k == 1)


def scalar(value):
    return jnp.reshape(value, (1,)).astype(jnp.int32)


def split_blocks(slab, place, replicas, *others):
    half = replicas // 2
    slab_rows, column_count = slab.shape[0], slab.shape[1] // replicas
    blocks = row_blocks(slab_rows)
    step = slab_rows // blocks

    def kernel(place_ref, slab_ref, *refs):
        keep_ref, send_ref = refs[-2:]
        parity = lax.rem(place_ref[0], 2)
        for j in range(half):
            for out_ref, own in ((keep_ref, parity), (send_ref, 1 - parity)):
                first = pl.multiple_of((2 * j + own) * column_count, column_count)
                out_ref[j] = slab_ref[:, pl.ds(first, column_count)]

    out = jax.ShapeDtypeStruct((half, slab_rows, column_count), slab.dtype)
    return call(
        kernel,
        vmem=TUNE.get("vo", 12),
        flops=int(TUNE.get("columns", 0) * 10**9),
        out_shape=[out, out],
        grid_spec=pltpu.PrefetchScalarGridSpec(
            num_scalar_prefetch=1,
            grid=(blocks,),
            in_specs=[pl.BlockSpec((step, slab.shape[1]), lambda i, place: (i, 0))]
            + [ANY] * len(others),
            out_specs=[pl.BlockSpec((half, step, column_count), lambda i, place: (0, i, 0))] * 2,
        ),
    )(scalar(place), slab, *others)


def pair_sums(keep, came, place, *others):
    half, slab_rows, column_count = keep.shape

    def kernel(place_ref, keep_ref, came_ref, *refs):
        outs = refs[-half:]
        mine = place_ref[0] // 2
        for j in range(half):
            k = mine ^ j
            outs[j][...] = keep_ref[k].astype(jnp.float32) + came_ref[k].astype(jnp.float32)

    out = jax.ShapeDtypeStruct((slab_rows, column_count), jnp.float32)
    whole = pl.BlockSpec(keep.shape, lambda i, place: (0, 0, 0))
    return call(
        kernel,
        vmem=14,
        out_shape=[out] * half,
        grid_spec=pltpu.PrefetchScalarGridSpec(
            num_scalar_prefetch=1,
            grid=(1,),
            in_specs=[whole, whole] + [ANY] * len(others),
            out_specs=[pl.BlockSpec(out.shape, lambda i, place: (0, 0))] * half,
        ),
    )(scalar(place), keep, came, *others)


def outer_update(parts, outer_params, outer_momentum, replicas, *others):
    def kernel(params_ref, momentum_ref, *refs):
        params_out, momentum_out = refs[-2:]
        summed = refs[0][...]
        for part in refs[1 : len(parts)]:
            summed = summed + part[...]
        average = summed / replicas
        params = params_ref[...]
        pseudo_grad = params - average
        new_momentum = OUTER_MOMENTUM * momentum_ref[...] + pseudo_grad
        momentum_out[...] = new_momentum
        params_out[...] = params - OUTER_RATE * (pseudo_grad + OUTER_MOMENTUM * new_momentum)

    whole = pl.BlockSpec(outer_params.shape, lambda: (0, 0))
    return call(
        kernel,
        vmem=12,
        out_shape=[shape_of(outer_params), shape_of(outer_momentum)],
        in_specs=[whole] * (2 + len(parts)) + [ANY] * len(others),
        out_specs=[whole] * 2,
    )(outer_params, outer_momentum, *parts, *others)


def merge(slab, mine, theirs, place):
    half, slab_rows, column_count = mine.shape
    blocks = row_blocks(slab_rows)
    step = slab_rows // blocks

    def kernel(place_ref, slab_ref, mine_ref, theirs_ref, out_ref):
        for j in range(half):
            for ref, owner in ((mine_ref, place_ref[0]), (theirs_ref, place_ref[0] ^ 1)):
                first = pl.multiple_of((owner ^ (2 * j)) * column_count, column_count)
                part = pl.ds(first, column_count)
                slab_f = slab_ref[:, part].astype(jnp.float32)
                merged = MERGE_WEIGHT * slab_f + (1.0 - MERGE_WEIGHT) * ref[j]
                out_ref[:, part] = merged.astype(out_ref.dtype)

    block = pl.BlockSpec((step, slab.shape[1]), lambda i, place: (i, 0))
    outer = pl.BlockSpec((half, step, column_count), lambda i, place: (0, i, 0))
    return call(
        kernel,
        vmem=TUNE.get("vm", 12),
        flops=int(TUNE.get("merge", 3) * 10**9),
        out_shape=shape_of(slab),
        grid_spec=pltpu.PrefetchScalarGridSpec(
            num_scalar_prefetch=1, grid=(blocks,), in_specs=[block, outer, outer], out_specs=block
        ),
    )(scalar(place), slab, mine, theirs)


def shards(
    tokens,
    key_cotangent,
    key_weight,
    first_moment,
    second_moment,
    local_slab,
    outer_params,
    outer_momentum,
):
    n = lax.axis_size("fsdp")
    me = lax.axis_index("fsdp")
    replicas = lax.axis_size("replica")
    rows = key_weight.shape[0]
    strip = rows // PIECES
    scale = term_scale(n * tokens.shape[0])
    every = range(PIECES)

    def mirrored(links):
        return [(n - 1 - a, n - 1 - b) for a, b in links]

    def among(devices):
        return functools.reduce(jnp.logical_or, [me == d for d in devices], jnp.bool_(False))

    def distinct(devices):
        return len(set(devices)) == len(devices)

    def exchange(up_load, down_load, up):
        down = mirrored(up)
        if distinct([a for a, _ in up + down]) and distinct([b for _, b in up + down]):
            load = up_load
            if up_load is not down_load:
                load = jnp.where(among([a for a, _ in up]), up_load, down_load)
            come = lax.ppermute(load, "fsdp", up + down)
            return come, come
        return lax.ppermute(up_load, "fsdp", up), lax.ppermute(down_load, "fsdp", down)

    def one_of(come):
        return come[0].astype(jnp.float32) if come[0] is come[1] else both(come)

    def both(come):
        return come[0].astype(jnp.float32) + come[1].astype(jnp.float32)

    weight_strip = rows // WEIGHT_PIECES
    each = range(WEIGHT_PIECES)
    weights = [key_weight[p * weight_strip : (p + 1) * weight_strip] for p in each]
    held = [[None] * WEIGHT_PIECES for _ in range(n)]
    sums = [None] * PIECES

    for p in each:
        held[0][p] = exchange(weights[p], weights[p], [(i, i + 1) for i in range(n - 1)])
    place = lax.axis_index("replica")

    def columns_of(owner, p):
        first = jnp.clip(owner, 0, n - 1) * rows + p * strip
        return lax.dynamic_slice_in_dim(tokens, first, strip, 1)

    def term(columns, cotangent):
        return scale * lax.dot_general(
            columns, cotangent, (((0,), (0,)), ((), ())), preferred_element_type=jnp.float32
        )

    if TUNE.get("gate") is not None:
        first_owner = jnp.where(me < 1, n + me - 1, 0 - (n - 1 - me))
        firsts = [after(term(columns_of(first_owner, q), key_cotangent)) for q in every]

    def swap(array, k):
        return lax.ppermute(array, "replica", [(i, i ^ k) for i in range(replicas)])

    late = tuple(firsts) if TUNE.get("late", 0) else ()
    keep, send = split_blocks(local_slab, place, replicas, *late)
    pairs = pair_sums(keep, swap(send, 1), place)
    parts = [pairs[0]] + [swap(pairs[j], 2 * j) for j in range(1, replicas // 2)]
    if TUNE.get("outer_tie") is not None:
        parts[0] = after(parts[0], *held[TUNE["outer_tie"]][0])
    new_outer, new_momentum = outer_update(parts, outer_params, outer_momentum, replicas)
    mine = [new_outer] + [swap(new_outer, 2 * j) for j in range(1, replicas // 2)]

    cotangent = key_cotangent
    for t in range(1, n):
        links = [(i, i + 1) for i in range(t)]
        up, down = n + me - t, t - 1 - (n - 1 - me)
        owners = [jnp.where(me < t, up, down)] if 2 * t <= n else [up, down]
        for p in every:
            w = p * WEIGHT_PIECES // PIECES
            if t == 1 and p == 0 and TUNE.get("gate") is not None:
                for v in each:
                    first = after(held[0][v][0], *firsts, flops=TUNE["gate"] * 10**9)
                    second = first if held[0][v][1] is held[0][v][0] else after(held[0][v][1], *firsts)
                    held[0][v] = (first, second)
            came = held[t - 1][w]
            if t < n - 1 and held[t][w] is None:
                held[t][w] = exchange(*came, [(i, i + 1) for i in range(t, n - 1)])
            if (t, p) == TUNE.get("mine_after"):
                mine[0] = after(mine[0], *came)
            extra = ()
            if (t, p) == TUNE.get("pairs_before"):
                extra = (pairs[0],)
            if (t, p) == TUNE.get("outer_before"):
                extra = (new_outer,)
            if (t, p) == TUNE.get("mine_before"):
                extra = tuple(mine[1:])
            tie = TUNE.get(("tie", t, p), t - 1)
            others = () if tie is None else tuple(held[tie][w])
            cost = TUNE.get(("x", t, p), 0) * 10**9
            source = cotangent if TUNE.get("chain", 0) else key_cotangent
            others = (*others, *extra)
            if others or cost:
                source = after(source, *others, flops=cost)
                cotangent = source
            if t == 1 and TUNE.get("gate") is not None:
                loads = [firsts[p]]
            else:
                loads = [term(columns_of(owner, p), source) for owner in owners]
            if len(loads) == 1:
                load = loads[0] if t == 1 else loads[0] + one_of(sums[p])
                up_load = down_load = load.astype(jnp.float16)
            else:
                up_load = (loads[0] + sums[p][0].astype(jnp.float32)).astype(jnp.float16)
                down_load = (loads[1] + sums[p][1].astype(jnp.float32)).astype(jnp.float16)
            sums[p] = exchange(up_load, down_load, links)

    mine = jnp.stack(mine)
    theirs = swap(mine, 1)
    new_local = merge(local_slab, mine, theirs, place)

    owners, valid, steps = [me], [me >= 0], [weights]
    for t in range(n - 1):
        if held[t][0][0] is held[t][0][1]:
            owners.append(jnp.where(me - t - 1 >= 0, me - t - 1, me + t + 1))
            valid.append((me - t - 1 >= 0) | (me + t + 1 <= n - 1))
            steps.append([held[t][p][0] for p in each])
        else:
            owners += [me - t - 1, me + t + 1]
            valid += [me - t - 1 >= 0, me + t + 1 <= n - 1]
            steps += [[held[t][p][0] for p in each], [held[t][p][1] for p in each]]
    owners = jnp.clip(jnp.stack(owners), 0, n - 1).astype(jnp.int32)
    others = (new_local,) if TUNE.get("merge_first", 1) else ()
    projected = project(owners, jnp.stack(valid).astype(jnp.int32), tokens, steps, rows, *others)

    source = after(key_cotangent, projected)
    own = [term(columns_of(me, p), source) for p in every]
    gradient = jnp.concatenate([own[p] + one_of(sums[p]) for p in every], 0) / scale
    new_first = BETA_ONE * first_moment + (1.0 - BETA_ONE) * gradient
    new_second = BETA_TWO * second_moment + (1.0 - BETA_TWO) * gradient * gradient
    weight_f = key_weight.astype(jnp.float32)
    update = (
        new_first / FIRST_FIX / (jnp.sqrt(new_second / SECOND_FIX) + EPSILON)
        + DECAY_RATE * weight_f
    )
    new_weight = (weight_f - INNER_RATE * update).astype(jnp.bfloat16)
    return (projected, new_weight, new_first, new_second, new_outer, new_momentum, new_local)


def solution(mesh):
    split = P(("replica", "fsdp"), None)
    outer = P("fsdp", "replica")
    return jax.shard_map(
        shards,
        mesh=mesh,
        in_specs=(split, split, split, split, split, split, outer, outer),
        out_specs=(split, split, split, split, outer, outer, split),
        check_vma=False,
    )
```

```python
import functools

import jax
import jax.numpy as jnp
from jax import lax
from jax.experimental import pallas as pl
from jax.experimental.pallas import tpu as pltpu
from jax.sharding import PartitionSpec as P

BETA_ONE = 0.9
BETA_TWO = 0.95
INNER_RATE = 0.001
DECAY_RATE = 0.1
EPSILON = 1e-08
FIRST_FIX = 1.0 - (0.9**50) ** 2
SECOND_FIX = 1.0 - (0.95**50) ** 2
OUTER_RATE = 0.7
OUTER_MOMENTUM = 0.9
MERGE_WEIGHT = 0.5
PIECES = 2
ANY = pl.BlockSpec(memory_space=pl.ANY)
MIB = 1 << 20


def term_scale(replica_tokens):
    scale = 1.0
    while replica_tokens * 6 * 0.25 * scale * 2 < 60000:
        scale *= 2
    return scale


def shape_of(array, dtype=None):
    return jax.ShapeDtypeStruct(array.shape, dtype or array.dtype)


def call(kernel, vmem, flops=0, **settings):
    return pl.pallas_call(
        kernel,
        compiler_params=pltpu.CompilerParams(vmem_limit_bytes=vmem * MIB),
        cost_estimate=pl.CostEstimate(flops=flops, bytes_accessed=0, transcendentals=0),
        **settings,
    )


def after(value, *others, flops=0):
    def kernel(*refs):
        pass

    return call(
        kernel,
        vmem=1,
        flops=flops,
        out_shape=shape_of(value),
        in_specs=[ANY] * (1 + len(others)),
        out_specs=ANY,
        input_output_aliases={0: 0},
    )(value, *others)


def copy_rows(array, strips, k, *others):
    strip = array.shape[0] // strips

    def kernel(in_ref, *refs):
        refs[-1][...] = in_ref[...]

    return call(
        kernel,
        vmem=8,
        out_shape=jax.ShapeDtypeStruct((strip, array.shape[1]), array.dtype),
        grid=(1,),
        in_specs=[pl.BlockSpec((strip, array.shape[1]), lambda i: (k, 0))] + [ANY] * len(others),
        out_specs=pl.BlockSpec((strip, array.shape[1]), lambda i: (0, 0)),
    )(array, *others)


def project(owners, valid, tokens, weights, rows, *others):
    strip, width = weights[0][0].shape
    strips = rows // strip
    steps = len(weights)
    flat = [piece for step in weights for piece in step]
    count = len(flat)

    def kernel(owners_ref, valid_ref, tokens_ref, *refs):
        out, total, held, sems = refs[-4:]
        step = pl.program_id(0)

        def copy(k, s):
            return pltpu.make_async_copy(refs[k * strips + s], held.at[k, s], sems.at[k, s])

        @pl.when(step == 0)
        def _():
            for k in range(steps):

                @pl.when(valid_ref[k] == 1)
                def _(k=k):
                    for s in range(strips):
                        copy(k, s).start()

            total[...] = jnp.zeros_like(total)

        @pl.when(valid_ref[step] == 1)
        def _():
            for s in range(strips):
                pltpu.make_async_copy(refs[s], held.at[step, s], sems.at[step, s]).wait()
                total[...] += jnp.dot(
                    tokens_ref[:, s * strip : (s + 1) * strip],
                    held[step, s],
                    preferred_element_type=jnp.float32,
                )

        @pl.when(step == steps - 1)
        def _():
            out[...] = total[...].astype(out.dtype)

    return call(
        kernel,
        vmem=16,
        flops=6 * 10**9,
        out_shape=jax.ShapeDtypeStruct((tokens.shape[0], width), jnp.bfloat16),
        grid_spec=pltpu.PrefetchScalarGridSpec(
            num_scalar_prefetch=2,
            grid=(steps,),
            in_specs=[pl.BlockSpec((tokens.shape[0], rows), lambda i, o, v: (0, o[i]))]
            + [ANY] * (count + len(others)),
            out_specs=pl.BlockSpec((tokens.shape[0], width), lambda i, o, v: (0, 0)),
            scratch_shapes=[
                pltpu.VMEM((tokens.shape[0], width), jnp.float32),
                pltpu.VMEM((steps, strips, strip, width), jnp.bfloat16),
                pltpu.SemaphoreType.DMA((steps, strips)),
            ],
        ),
    )(owners, valid, tokens, *flat, *others)


def row_blocks(slab_rows):
    return next(k for k in (4, 3, 2, 1) if slab_rows % (16 * k) == 0 or k == 1)


def scalar(value):
    return jnp.reshape(value, (1,)).astype(jnp.int32)


def split_blocks(slab, place, replicas, *others):
    half = replicas // 2
    slab_rows, column_count = slab.shape[0], slab.shape[1] // replicas
    blocks = row_blocks(slab_rows)
    step = slab_rows // blocks

    def kernel(place_ref, slab_ref, *refs):
        keep_ref, send_ref = refs[-2:]
        parity = lax.rem(place_ref[0], 2)
        for j in range(half):
            for out_ref, own in ((keep_ref, parity), (send_ref, 1 - parity)):
                first = pl.multiple_of((2 * j + own) * column_count, column_count)
                out_ref[j] = slab_ref[:, pl.ds(first, column_count)]

    out = jax.ShapeDtypeStruct((half, slab_rows, column_count), slab.dtype)
    return call(
        kernel,
        vmem=12,
        out_shape=[out, out],
        grid_spec=pltpu.PrefetchScalarGridSpec(
            num_scalar_prefetch=1,
            grid=(blocks,),
            in_specs=[pl.BlockSpec((step, slab.shape[1]), lambda i, place: (i, 0))]
            + [ANY] * len(others),
            out_specs=[pl.BlockSpec((half, step, column_count), lambda i, place: (0, i, 0))] * 2,
        ),
    )(scalar(place), slab, *others)


def pair_sums(keep, came, place, *others):
    half, slab_rows, column_count = keep.shape

    def kernel(place_ref, keep_ref, came_ref, *refs):
        outs = refs[-half:]
        mine = place_ref[0] // 2
        for j in range(half):
            k = mine ^ j
            outs[j][...] = keep_ref[k].astype(jnp.float32) + came_ref[k].astype(jnp.float32)

    out = jax.ShapeDtypeStruct((slab_rows, column_count), jnp.float32)
    whole = pl.BlockSpec(keep.shape, lambda i, place: (0, 0, 0))
    return call(
        kernel,
        vmem=14,
        out_shape=[out] * half,
        grid_spec=pltpu.PrefetchScalarGridSpec(
            num_scalar_prefetch=1,
            grid=(1,),
            in_specs=[whole, whole] + [ANY] * len(others),
            out_specs=[pl.BlockSpec(out.shape, lambda i, place: (0, 0))] * half,
        ),
    )(scalar(place), keep, came, *others)


def outer_update(parts, outer_params, outer_momentum, replicas, *others):
    def kernel(params_ref, momentum_ref, *refs):
        params_out, momentum_out = refs[-2:]
        summed = refs[0][...]
        for part in refs[1 : len(parts)]:
            summed = summed + part[...]
        average = summed / replicas
        params = params_ref[...]
        pseudo_grad = params - average
        new_momentum = OUTER_MOMENTUM * momentum_ref[...] + pseudo_grad
        momentum_out[...] = new_momentum
        params_out[...] = params - OUTER_RATE * (pseudo_grad + OUTER_MOMENTUM * new_momentum)

    whole = pl.BlockSpec(outer_params.shape, lambda: (0, 0))
    return call(
        kernel,
        vmem=12,
        out_shape=[shape_of(outer_params), shape_of(outer_momentum)],
        in_specs=[whole] * (2 + len(parts)) + [ANY] * len(others),
        out_specs=[whole] * 2,
    )(outer_params, outer_momentum, *parts, *others)


def merge(slab, mine, theirs, place):
    half, slab_rows, column_count = mine.shape
    blocks = row_blocks(slab_rows)
    step = slab_rows // blocks

    def kernel(place_ref, slab_ref, mine_ref, theirs_ref, out_ref):
        for j in range(half):
            for ref, owner in ((mine_ref, place_ref[0]), (theirs_ref, place_ref[0] ^ 1)):
                first = pl.multiple_of((owner ^ (2 * j)) * column_count, column_count)
                part = pl.ds(first, column_count)
                slab_f = slab_ref[:, part].astype(jnp.float32)
                merged = MERGE_WEIGHT * slab_f + (1.0 - MERGE_WEIGHT) * ref[j]
                out_ref[:, part] = merged.astype(out_ref.dtype)

    block = pl.BlockSpec((step, slab.shape[1]), lambda i, place: (i, 0))
    outer = pl.BlockSpec((half, step, column_count), lambda i, place: (0, i, 0))
    return call(
        kernel,
        vmem=12,
        flops=3 * 10**9,
        out_shape=shape_of(slab),
        grid_spec=pltpu.PrefetchScalarGridSpec(
            num_scalar_prefetch=1, grid=(blocks,), in_specs=[block, outer, outer], out_specs=block
        ),
    )(scalar(place), slab, mine, theirs)


def shards(
    tokens,
    key_cotangent,
    key_weight,
    first_moment,
    second_moment,
    local_slab,
    outer_params,
    outer_momentum,
):
    n = lax.axis_size("fsdp")
    me = lax.axis_index("fsdp")
    replicas = lax.axis_size("replica")
    rows = key_weight.shape[0]
    strip = rows // PIECES
    scale = term_scale(n * tokens.shape[0])
    every = range(PIECES)

    def mirrored(links):
        return [(n - 1 - a, n - 1 - b) for a, b in links]

    def among(devices):
        return functools.reduce(jnp.logical_or, [me == d for d in devices], jnp.bool_(False))

    def distinct(devices):
        return len(set(devices)) == len(devices)

    def exchange(up_load, down_load, up):
        down = mirrored(up)
        if distinct([a for a, _ in up + down]) and distinct([b for _, b in up + down]):
            load = up_load
            if up_load is not down_load:
                load = jnp.where(among([a for a, _ in up]), up_load, down_load)
            come = lax.ppermute(load, "fsdp", up + down)
            return come, come
        return lax.ppermute(up_load, "fsdp", up), lax.ppermute(down_load, "fsdp", down)

    def one_of(come):
        return come[0].astype(jnp.float32) if come[0] is come[1] else both(come)

    def both(come):
        return come[0].astype(jnp.float32) + come[1].astype(jnp.float32)

    weights = [copy_rows(key_weight, PIECES, p) for p in every]
    held = [[None] * PIECES for _ in range(n)]
    sums = [None] * PIECES
    for p in every:
        held[0][p] = exchange(weights[p], weights[p], [(i, i + 1) for i in range(n - 1)])
    place = lax.axis_index("replica")

    def columns_of(owner, p):
        first = jnp.clip(owner, 0, n - 1) * rows + p * strip
        return lax.dynamic_slice_in_dim(tokens, first, strip, 1)

    def term(columns, cotangent):
        return scale * lax.dot_general(
            columns, cotangent, (((0,), (0,)), ((), ())), preferred_element_type=jnp.float32
        )

    def swap(array, k):
        return lax.ppermute(array, "replica", [(i, i ^ k) for i in range(replicas)])

    keep, send = split_blocks(local_slab, place, replicas)
    pairs = pair_sums(keep, swap(send, 1), place)
    parts = [pairs[0]] + [swap(pairs[j], 2 * j) for j in range(1, replicas // 2)]
    new_outer, new_momentum = outer_update(parts, outer_params, outer_momentum, replicas)
    mine = [new_outer] + [swap(new_outer, 2 * j) for j in range(1, replicas // 2)]

    cotangent = copy_rows(key_cotangent, 1, 0, held[0][0][0])
    for t in range(1, n):
        links = [(i, i + 1) for i in range(t)]
        up, down = n + me - t, t - 1 - (n - 1 - me)
        owners = [jnp.where(me < t, up, down)] if 2 * t <= n else [up, down]
        for p in every:
            came = held[t - 1][p]
            if t < n - 1:
                held[t][p] = exchange(*came, [(i, i + 1) for i in range(t, n - 1)])
            source = key_cotangent
            if t > 1:
                source = cotangent = after(cotangent, *held[t - 1][p], flops=14 * 10**9)
            if t == n - 1 and p == 0:
                mine = [mine[0]] + [after(block, source) for block in mine[1:]]
            loads = [term(columns_of(owner, p), source) for owner in owners]
            if len(loads) == 1:
                load = loads[0] if t == 1 else loads[0] + one_of(sums[p])
                up_load = down_load = load.astype(jnp.float16)
            else:
                up_load = (loads[0] + sums[p][0].astype(jnp.float32)).astype(jnp.float16)
                down_load = (loads[1] + sums[p][1].astype(jnp.float32)).astype(jnp.float16)
            sums[p] = exchange(up_load, down_load, links)

    mine = jnp.stack(mine)
    theirs = swap(mine, 1)
    new_local = merge(local_slab, mine, theirs, place)

    owners, valid, steps = [me], [me >= 0], [weights]
    for t in range(n - 1):
        if held[t][0][0] is held[t][0][1]:
            owners.append(jnp.where(me - t - 1 >= 0, me - t - 1, me + t + 1))
            valid.append((me - t - 1 >= 0) | (me + t + 1 <= n - 1))
            steps.append([held[t][p][0] for p in every])
        else:
            owners += [me - t - 1, me + t + 1]
            valid += [me - t - 1 >= 0, me + t + 1 <= n - 1]
            steps += [[held[t][p][0] for p in every], [held[t][p][1] for p in every]]
    owners = jnp.clip(jnp.stack(owners), 0, n - 1).astype(jnp.int32)
    valid = jnp.stack(valid).astype(jnp.int32)
    projected = project(owners, valid, tokens, steps, rows, new_local)

    source = after(cotangent, projected)
    own = [term(columns_of(me, p), source) for p in every]
    gradient = jnp.concatenate([own[p] + one_of(sums[p]) for p in every], 0) / scale
    new_first = BETA_ONE * first_moment + (1.0 - BETA_ONE) * gradient
    new_second = BETA_TWO * second_moment + (1.0 - BETA_TWO) * gradient * gradient
    weight_f = key_weight.astype(jnp.float32)
    update = (
        new_first / FIRST_FIX / (jnp.sqrt(new_second / SECOND_FIX) + EPSILON)
        + DECAY_RATE * weight_f
    )
    new_weight = (weight_f - INNER_RATE * update).astype(jnp.bfloat16)
    return (projected, new_weight, new_first, new_second, new_outer, new_momentum, new_local)


def solution(mesh):
    split = P(("replica", "fsdp"), None)
    outer = P("fsdp", "replica")
    return jax.shard_map(
        shards,
        mesh=mesh,
        in_specs=(split, split, split, split, split, split, outer, outer),
        out_specs=(split, split, split, split, outer, outer, split),
        check_vma=False,
    )
```

```python
import functools

import jax
import jax.numpy as jnp
from jax import lax
from jax.experimental import pallas as pl
from jax.experimental.pallas import tpu as pltpu
from jax.sharding import PartitionSpec as P

BETA_ONE = 0.9
BETA_TWO = 0.95
INNER_RATE = 0.001
DECAY_RATE = 0.1
EPSILON = 1e-08
FIRST_FIX = 1.0 - (0.9**50) ** 2
SECOND_FIX = 1.0 - (0.95**50) ** 2
OUTER_RATE = 0.7
OUTER_MOMENTUM = 0.9
MERGE_WEIGHT = 0.5
PIECES = 2
ANY = pl.BlockSpec(memory_space=pl.ANY)
MIB = 1 << 20


def term_scale(replica_tokens):
    scale = 1.0
    while replica_tokens * 6 * 0.25 * scale * 2 < 60000:
        scale *= 2
    return scale


def shape_of(array, dtype=None):
    return jax.ShapeDtypeStruct(array.shape, dtype or array.dtype)


def call(kernel, vmem, flops=0, **settings):
    return pl.pallas_call(
        kernel,
        compiler_params=pltpu.CompilerParams(vmem_limit_bytes=vmem * MIB),
        cost_estimate=pl.CostEstimate(flops=flops, bytes_accessed=0, transcendentals=0),
        **settings,
    )


def after(value, *others, flops=0):
    def kernel(*refs):
        pass

    return call(
        kernel,
        vmem=1,
        flops=flops,
        out_shape=shape_of(value),
        in_specs=[ANY] * (1 + len(others)),
        out_specs=ANY,
        input_output_aliases={0: 0},
    )(value, *others)


def copy_rows(array, strips, k, *others):
    strip = array.shape[0] // strips

    def kernel(in_ref, *refs):
        refs[-1][...] = in_ref[...]

    return call(
        kernel,
        vmem=8,
        out_shape=jax.ShapeDtypeStruct((strip, array.shape[1]), array.dtype),
        grid=(1,),
        in_specs=[pl.BlockSpec((strip, array.shape[1]), lambda i: (k, 0))] + [ANY] * len(others),
        out_specs=pl.BlockSpec((strip, array.shape[1]), lambda i: (0, 0)),
    )(array, *others)


def project(owners, valid, tokens, weights, rows, *others):
    strip, width = weights[0][0].shape
    strips = rows // strip
    steps = len(weights)
    flat = [piece for step in weights for piece in step]
    count = len(flat)

    def kernel(owners_ref, valid_ref, tokens_ref, *refs):
        out, total, held, sems = refs[-4:]
        step = pl.program_id(0)

        def copy(k, s):
            return pltpu.make_async_copy(refs[k * strips + s], held.at[k, s], sems.at[k, s])

        @pl.when(step == 0)
        def _():
            for k in range(steps):

                @pl.when(valid_ref[k] == 1)
                def _(k=k):
                    for s in range(strips):
                        copy(k, s).start()

            total[...] = jnp.zeros_like(total)

        @pl.when(valid_ref[step] == 1)
        def _():
            for s in range(strips):
                pltpu.make_async_copy(refs[s], held.at[step, s], sems.at[step, s]).wait()
                total[...] += jnp.dot(
                    tokens_ref[:, s * strip : (s + 1) * strip],
                    held[step, s],
                    preferred_element_type=jnp.float32,
                )

        @pl.when(step == steps - 1)
        def _():
            out[...] = total[...].astype(out.dtype)

    return call(
        kernel,
        vmem=16,
        flops=6 * 10**9,
        out_shape=jax.ShapeDtypeStruct((tokens.shape[0], width), jnp.bfloat16),
        grid_spec=pltpu.PrefetchScalarGridSpec(
            num_scalar_prefetch=2,
            grid=(steps,),
            in_specs=[pl.BlockSpec((tokens.shape[0], rows), lambda i, o, v: (0, o[i]))]
            + [ANY] * (count + len(others)),
            out_specs=pl.BlockSpec((tokens.shape[0], width), lambda i, o, v: (0, 0)),
            scratch_shapes=[
                pltpu.VMEM((tokens.shape[0], width), jnp.float32),
                pltpu.VMEM((steps, strips, strip, width), jnp.bfloat16),
                pltpu.SemaphoreType.DMA((steps, strips)),
            ],
        ),
    )(owners, valid, tokens, *flat, *others)


def row_blocks(slab_rows):
    return next(k for k in (4, 3, 2, 1) if slab_rows % (16 * k) == 0 or k == 1)


def scalar(value):
    return jnp.reshape(value, (1,)).astype(jnp.int32)


def split_blocks(slab, place, replicas, *others):
    half = replicas // 2
    slab_rows, column_count = slab.shape[0], slab.shape[1] // replicas
    blocks = row_blocks(slab_rows)
    step = slab_rows // blocks

    def kernel(place_ref, slab_ref, *refs):
        keep_ref, send_ref = refs[-2:]
        parity = lax.rem(place_ref[0], 2)
        for j in range(half):
            for out_ref, own in ((keep_ref, parity), (send_ref, 1 - parity)):
                first = pl.multiple_of((2 * j + own) * column_count, column_count)
                out_ref[j] = slab_ref[:, pl.ds(first, column_count)]

    out = jax.ShapeDtypeStruct((half, slab_rows, column_count), slab.dtype)
    return call(
        kernel,
        vmem=12,
        out_shape=[out, out],
        grid_spec=pltpu.PrefetchScalarGridSpec(
            num_scalar_prefetch=1,
            grid=(blocks,),
            in_specs=[pl.BlockSpec((step, slab.shape[1]), lambda i, place: (i, 0))]
            + [ANY] * len(others),
            out_specs=[pl.BlockSpec((half, step, column_count), lambda i, place: (0, i, 0))] * 2,
        ),
    )(scalar(place), slab, *others)


def pair_sums(keep, came, place, *others):
    half, slab_rows, column_count = keep.shape

    def kernel(place_ref, keep_ref, came_ref, *refs):
        outs = refs[-half:]
        mine = place_ref[0] // 2
        for j in range(half):
            k = mine ^ j
            outs[j][...] = keep_ref[k].astype(jnp.float32) + came_ref[k].astype(jnp.float32)

    out = jax.ShapeDtypeStruct((slab_rows, column_count), jnp.float32)
    whole = pl.BlockSpec(keep.shape, lambda i, place: (0, 0, 0))
    return call(
        kernel,
        vmem=14,
        out_shape=[out] * half,
        grid_spec=pltpu.PrefetchScalarGridSpec(
            num_scalar_prefetch=1,
            grid=(1,),
            in_specs=[whole, whole] + [ANY] * len(others),
            out_specs=[pl.BlockSpec(out.shape, lambda i, place: (0, 0))] * half,
        ),
    )(scalar(place), keep, came, *others)


def outer_update(parts, outer_params, outer_momentum, replicas, *others):
    def kernel(params_ref, momentum_ref, *refs):
        params_out, momentum_out = refs[-2:]
        summed = refs[0][...]
        for part in refs[1 : len(parts)]:
            summed = summed + part[...]
        average = summed / replicas
        params = params_ref[...]
        pseudo_grad = params - average
        new_momentum = OUTER_MOMENTUM * momentum_ref[...] + pseudo_grad
        momentum_out[...] = new_momentum
        params_out[...] = params - OUTER_RATE * (pseudo_grad + OUTER_MOMENTUM * new_momentum)

    whole = pl.BlockSpec(outer_params.shape, lambda: (0, 0))
    return call(
        kernel,
        vmem=12,
        out_shape=[shape_of(outer_params), shape_of(outer_momentum)],
        in_specs=[whole] * (2 + len(parts)) + [ANY] * len(others),
        out_specs=[whole] * 2,
    )(outer_params, outer_momentum, *parts, *others)


def merge(slab, mine, theirs, place):
    half, slab_rows, column_count = mine.shape
    blocks = row_blocks(slab_rows)
    step = slab_rows // blocks

    def kernel(place_ref, slab_ref, mine_ref, theirs_ref, out_ref):
        for j in range(half):
            for ref, owner in ((mine_ref, place_ref[0]), (theirs_ref, place_ref[0] ^ 1)):
                first = pl.multiple_of((owner ^ (2 * j)) * column_count, column_count)
                part = pl.ds(first, column_count)
                slab_f = slab_ref[:, part].astype(jnp.float32)
                merged = MERGE_WEIGHT * slab_f + (1.0 - MERGE_WEIGHT) * ref[j]
                out_ref[:, part] = merged.astype(out_ref.dtype)

    block = pl.BlockSpec((step, slab.shape[1]), lambda i, place: (i, 0))
    outer = pl.BlockSpec((half, step, column_count), lambda i, place: (0, i, 0))
    return call(
        kernel,
        vmem=12,
        flops=3 * 10**9,
        out_shape=shape_of(slab),
        grid_spec=pltpu.PrefetchScalarGridSpec(
            num_scalar_prefetch=1, grid=(blocks,), in_specs=[block, outer, outer], out_specs=block
        ),
    )(scalar(place), slab, mine, theirs)


def shards(
    tokens,
    key_cotangent,
    key_weight,
    first_moment,
    second_moment,
    local_slab,
    outer_params,
    outer_momentum,
):
    n = lax.axis_size("fsdp")
    me = lax.axis_index("fsdp")
    replicas = lax.axis_size("replica")
    rows = key_weight.shape[0]
    strip = rows // PIECES
    scale = term_scale(n * tokens.shape[0])
    every = range(PIECES)

    def mirrored(links):
        return [(n - 1 - a, n - 1 - b) for a, b in links]

    def among(devices):
        return functools.reduce(jnp.logical_or, [me == d for d in devices], jnp.bool_(False))

    def distinct(devices):
        return len(set(devices)) == len(devices)

    def exchange(up_load, down_load, up):
        down = mirrored(up)
        if distinct([a for a, _ in up + down]) and distinct([b for _, b in up + down]):
            load = up_load
            if up_load is not down_load:
                load = jnp.where(among([a for a, _ in up]), up_load, down_load)
            come = lax.ppermute(load, "fsdp", up + down)
            return come, come
        return lax.ppermute(up_load, "fsdp", up), lax.ppermute(down_load, "fsdp", down)

    def one_of(come):
        return come[0].astype(jnp.float32) if come[0] is come[1] else both(come)

    def both(come):
        return come[0].astype(jnp.float32) + come[1].astype(jnp.float32)

    weights = [copy_rows(key_weight, PIECES, p) for p in every]
    held = [[None] * PIECES for _ in range(n)]
    sums = [None] * PIECES
    for p in every:
        held[0][p] = exchange(weights[p], weights[p], [(i, i + 1) for i in range(n - 1)])
    place = lax.axis_index("replica")

    def columns_of(owner, p):
        first = jnp.clip(owner, 0, n - 1) * rows + p * strip
        return lax.dynamic_slice_in_dim(tokens, first, strip, 1)

    def term(columns, cotangent):
        return scale * lax.dot_general(
            columns, cotangent, (((0,), (0,)), ((), ())), preferred_element_type=jnp.float32
        )

    def swap(array, k):
        return lax.ppermute(array, "replica", [(i, i ^ k) for i in range(replicas)])

    keep, send = split_blocks(local_slab, place, replicas, held[0][0][0])
    pairs = pair_sums(keep, swap(send, 1), place)
    parts = [pairs[0]] + [swap(pairs[j], 2 * j) for j in range(1, replicas // 2)]
    new_outer, new_momentum = outer_update(parts, outer_params, outer_momentum, replicas)
    mine = [new_outer] + [swap(new_outer, 2 * j) for j in range(1, replicas // 2)]

    cotangent = copy_rows(key_cotangent, 1, 0, held[0][0][0])
    for t in range(1, n):
        links = [(i, i + 1) for i in range(t)]
        up, down = n + me - t, t - 1 - (n - 1 - me)
        owners = [jnp.where(me < t, up, down)] if 2 * t <= n else [up, down]
        for p in every:
            came = held[t - 1][p]
            if t < n - 1:
                held[t][p] = exchange(*came, [(i, i + 1) for i in range(t, n - 1)])
            source = key_cotangent
            if t > 1:
                source = cotangent = after(cotangent, *held[t - 1][p], flops=14 * 10**9)
            if t == n - 1 and p == 0:
                mine = [mine[0]] + [after(block, source) for block in mine[1:]]
            loads = [term(columns_of(owner, p), source) for owner in owners]
            if len(loads) == 1:
                load = loads[0] if t == 1 else loads[0] + one_of(sums[p])
                up_load = down_load = load.astype(jnp.float16)
            else:
                up_load = (loads[0] + sums[p][0].astype(jnp.float32)).astype(jnp.float16)
                down_load = (loads[1] + sums[p][1].astype(jnp.float32)).astype(jnp.float16)
            sums[p] = exchange(up_load, down_load, links)

    mine = jnp.stack(mine)
    theirs = swap(mine, 1)
    new_local = merge(local_slab, mine, theirs, place)

    owners, valid, steps = [me], [me >= 0], [weights]
    for t in range(n - 1):
        if held[t][0][0] is held[t][0][1]:
            owners.append(jnp.where(me - t - 1 >= 0, me - t - 1, me + t + 1))
            valid.append((me - t - 1 >= 0) | (me + t + 1 <= n - 1))
            steps.append([held[t][p][0] for p in every])
        else:
            owners += [me - t - 1, me + t + 1]
            valid += [me - t - 1 >= 0, me + t + 1 <= n - 1]
            steps += [[held[t][p][0] for p in every], [held[t][p][1] for p in every]]
    owners = jnp.clip(jnp.stack(owners), 0, n - 1).astype(jnp.int32)
    valid = jnp.stack(valid).astype(jnp.int32)
    projected = project(owners, valid, tokens, steps, rows, new_local)

    source = after(cotangent, projected)
    own = [term(columns_of(me, p), source) for p in every]
    gradient = jnp.concatenate([own[p] + one_of(sums[p]) for p in every], 0) / scale
    new_first = BETA_ONE * first_moment + (1.0 - BETA_ONE) * gradient
    new_second = BETA_TWO * second_moment + (1.0 - BETA_TWO) * gradient * gradient
    weight_f = key_weight.astype(jnp.float32)
    update = (
        new_first / FIRST_FIX / (jnp.sqrt(new_second / SECOND_FIX) + EPSILON)
        + DECAY_RATE * weight_f
    )
    new_weight = (weight_f - INNER_RATE * update).astype(jnp.bfloat16)
    return (projected, new_weight, new_first, new_second, new_outer, new_momentum, new_local)


def solution(mesh):
    split = P(("replica", "fsdp"), None)
    outer = P("fsdp", "replica")
    return jax.shard_map(
        shards,
        mesh=mesh,
        in_specs=(split, split, split, split, split, split, outer, outer),
        out_specs=(split, split, split, split, outer, outer, split),
        check_vma=False,
    )
```
